32 devices in a mesh: groups: 2 (over x), own: 8 (over z, y), sub: 2 (over core).
Axes of the slice: x: 2, y: 2, z: 4, core: 2. Of those that a mesh axis runs over, the one named last changes fastest.
Arguments:
- embeddings: bfloat16 [24576, 1024], P(('groups', 'own', 'sub')), parts along dimension 0, may hold values from -4000 to 4000
- cluster_ids: int32 [24576], P(('groups', 'own', 'sub')), parts along dimension 0, may hold values from 0 to 15, as said below
- valid_counts: int32 [32], P(('groups', 'own', 'sub')), parts along dimension 0, may hold values from 576 to 768, as said below
Outputs:
- nearest: float32 [24576], P(('groups', 'own', 'sub')), parts along dimension 0
The draws below stay inside these ranges and needn't reach their ends.
There are 2 independent parts, one for each index of `groups`. The reference program is written for one: setup_inputs(seed, part) draws one part's arguments, and reference() takes and returns one part's arrays. A program takes and returns all parts, laid end to end along the dimension named above; each array names one. Nothing has to cross between parts.
Inputs may be any that keep to these rules, and one draw needn't show every extreme that they name: `cluster_ids`: cluster c belongs to owner c // 2. Among the valid rows of one device at most 192 lie in the clusters of one owner, and in every draw some owner gets exactly 192 valid rows from every device, so that the clusters of that owner together hold 3072 valid rows, the most that any owner's clusters hold. `valid_counts`: some device is full in every draw.
All inputs are finite; a program needn't handle non-finite values.
Results may differ from the reference program's by a relative error of at most 0.00053.
Values may be sent and summed in bfloat16 or wider, within the bound.
No kernel may reach another device: no remote copies, remote signals or barrier semaphores. Data moves between devices by JAX's collectives and lax.ppermute only.
A program may use at most 64 MiB of HBM per device.

```python
import math
import jax
import jax.numpy as jnp
from jax import lax

D = 1024
ROW_DEV = 768
CL_OWN = 2
DUPS = 256
DEVS = 16
ROWS = 12288
CAP = 192
CLUSTERS = 16
N_OWN = 8


def layout(key):
    position_count = N_OWN * CAP
    heavy_key, forced_key, device_key = jax.random.split(key, 3)
    weighty_cluster = jax.random.randint(heavy_key, (N_OWN,), 0, 4)
    compelled_choice = jax.random.randint(forced_key, (), 0, N_OWN)

    def one_device(dev_key):
        key_one, key_two, key_three, key_four, key_five = jax.random.split(dev_key, 5)
        position_index = jnp.arange(position_count, dtype=jnp.int32)
        position_holder = position_index // CAP
        random_jitter = jax.random.randint(key_one, (position_count,), 0, 4096)
        extra_reward = 4096 * weighty_cluster[position_holder] + 16384 * (position_holder == compelled_choice).astype(jnp.int32)
        match_score = (random_jitter + extra_reward) * position_count + position_index
        top_values, picked = lax.top_k(match_score, ROW_DEV)
        half_count = ROW_DEV // 2
        first_part = picked[:half_count][jax.random.permutation(key_two, half_count)]
        second_part = picked[half_count:][jax.random.permutation(key_three, ROW_DEV - half_count)]
        chosen = jnp.concatenate([first_part, second_part]).astype(jnp.int32)
        row_owner = chosen // CAP
        cluster = row_owner * CL_OWN + jax.random.randint(key_four, (ROW_DEV,), 0, CL_OWN)
        source = jax.random.randint(key_five, (ROW_DEV,), 0, DUPS)
        return (cluster.astype(jnp.int32), source.astype(jnp.int32))
    dev_keys = jax.vmap(lambda index: jax.random.fold_in(device_key, index))(jnp.arange(DEVS))
    cluster, source = jax.vmap(one_device)(dev_keys)
    return (cluster.reshape(-1), source.reshape(-1))


def draw_cluster_ids(key, part):
    cluster, source = layout(key)
    return cluster


def draw_embeddings(key, part):
    cluster, source = layout(key)
    key = jax.random.fold_in(key, 7)
    center_key, shared_key, own_key, row_key, col_key = jax.random.split(key, 5)
    centers = jax.random.normal(center_key, (CLUSTERS, D), jnp.float32)
    shared = jax.random.normal(shared_key, (CLUSTERS * DUPS, D), jnp.float32)
    own_part = jax.random.normal(own_key, (ROWS, D), jnp.float32)
    row_scale = jnp.exp(jax.random.uniform(row_key, (ROWS, 1), jnp.float32, 0.0, math.log(10.0)))
    col_scale = jnp.exp(jax.random.uniform(col_key, (1, D), jnp.float32, math.log(0.5), math.log(2.0)))
    mixed = 0.8 * centers[cluster] + shared[cluster * DUPS + source] + 0.45 * own_part
    mixed = jnp.clip(mixed * col_scale * row_scale, -4000.0, 4000.0)
    return mixed.astype(jnp.bfloat16)


def draw_valid_counts(key, part):
    key = jax.random.fold_in(key, 11)
    count_key, full_key = jax.random.split(key)
    counts = jax.random.randint(count_key, (DEVS,), 3 * ROW_DEV // 4, ROW_DEV + 1)
    full_index = jax.random.randint(full_key, (), 0, DEVS)
    counts = counts.at[full_index].set(ROW_DEV)
    return counts.astype(jnp.int32)


def setup_inputs(seed: int = 0, part: int = 0) -> dict:
    keys = jax.random.split(jax.random.key(seed), 4)
    part_splits = jax.random.split(jax.random.fold_in(keys[3], part), 4)
    return {
        "embeddings": draw_embeddings(jax.random.fold_in(jax.random.fold_in(keys[3], part), 71), part),
        "cluster_ids": draw_cluster_ids(jax.random.fold_in(jax.random.fold_in(keys[3], part), 71), part),
        "valid_counts": draw_valid_counts(jax.random.fold_in(jax.random.fold_in(keys[3], part), 71), part),
    }


epsilon = 1e-06

def reference(embeddings, cluster_ids, valid_counts):
    row_count = embeddings.shape[0]
    position = jnp.arange(row_count, dtype=jnp.int32)
    is_valid = position % ROW_DEV < valid_counts[position // ROW_DEV]
    widened = embeddings.astype(jnp.float32)
    unit_rows = (widened * lax.rsqrt(lax.optimization_barrier(jnp.sum(widened * widened, axis=1, keepdims=True)) + epsilon)).astype(jnp.bfloat16)
    group = jnp.where(is_valid, cluster_ids, -1).astype(jnp.int32)
    order = jnp.argsort(group, stable=True).astype(jnp.int32)
    sorted_rows = unit_rows[order].astype(jnp.float32)
    sorted_group = group[order]
    cluster_start = jnp.searchsorted(sorted_group, sorted_group, side='left').astype(jnp.int32)
    block_size = min(256, row_count)
    span = block_size + 8 * ROW_DEV
    padded_rows = jnp.concatenate([sorted_rows, jnp.zeros((span, D), jnp.float32)], axis=0)
    padded_group = jnp.concatenate([sorted_group, jnp.full((span,), -2, jnp.int32)], axis=0)

    def score_block(block_start):
        queries = lax.dynamic_slice_in_dim(sorted_rows, block_start, block_size, 0)
        query_group = lax.dynamic_slice_in_dim(sorted_group, block_start, block_size, 0)
        first_group = sorted_group[block_start]
        window_start = jnp.where(first_group < 0, block_start, cluster_start[block_start]).astype(jnp.int32)
        key_rows = lax.dynamic_slice_in_dim(padded_rows, window_start, span, 0)
        key_group = lax.dynamic_slice_in_dim(padded_group, window_start, span, 0)
        scores = jnp.dot(queries, key_rows.T, precision=lax.Precision.HIGHEST, preferred_element_type=jnp.float32)
        query_pos = block_start + jnp.arange(block_size, dtype=jnp.int32)
        key_pos = window_start + jnp.arange(span, dtype=jnp.int32)
        pair_mask = (query_group[:, None] == key_group[None, :]) & (query_group[:, None] >= 0) & (query_pos[:, None] != key_pos[None, :])
        return lax.optimization_barrier(jnp.max(jnp.where(pair_mask, scores, -1.0), axis=1))
    starts = jnp.arange(row_count // block_size, dtype=jnp.int32) * block_size
    best_sorted = lax.map(score_block, starts).reshape(-1)
    nearest = jnp.zeros((row_count,), jnp.float32).at[order].set(best_sorted)
    return jnp.where(is_valid, nearest, 0.0)
```

```python
import jax
import jax.numpy as jnp
from jax import lax
from jax.experimental import pallas as pl
from jax.experimental.pallas import tpu as pltpu
from jax.sharding import PartitionSpec as P

CL_OWN = 2
epsilon = 1e-06

F32 = jnp.float32
BF16 = jnp.bfloat16
I32 = jnp.int32
VMEM_LIMIT = 48 * 1024 * 1024


def vmem():
    return pl.BlockSpec(memory_space=pltpu.VMEM)


def smem():
    return pl.BlockSpec(memory_space=pltpu.SMEM)


def hbm():
    return pl.BlockSpec(memory_space=pl.ANY)


def group_index():
    return lax.axis_index("own") * 2 + lax.axis_index("sub")


def count_kernel(ids_ref, valid_ref, out_ref):
    clusters, lanes = out_ref.shape
    rows = ids_ref.shape[1]
    is_valid = lax.broadcasted_iota(I32, (1, rows), 1) < valid_ref[0]
    hit = (ids_ref[...] == lax.broadcasted_iota(I32, (clusters, rows), 0)) & is_valid
    total = jnp.sum(hit.astype(F32), axis=1, keepdims=True).astype(I32)
    mine = lax.broadcasted_iota(I32, (clusters, lanes), 1) == group_index()
    out_ref[...] = jnp.where(mine, total, 0)


def plan_kernel(planes, caps, counts_ref, plane_ref, tier_ref):
    clusters = counts_ref.shape[0]
    owners = clusters // CL_OWN
    counts = counts_ref[...].astype(F32)
    rows = [counts[c : c + 1] for c in range(clusters)]
    keys = []
    for o in range(owners):
        both = rows[o * CL_OWN]
        for k in range(1, CL_OWN):
            both = both + rows[o * CL_OWN + k]
        keys.append(jnp.max(both))
    loads = [F32(0.0)] * planes
    place = [I32(0)] * owners
    for _ in range(owners):
        best, best_at = keys[0], I32(0)
        for o in range(1, owners):
            more = keys[o] > best
            best = jnp.where(more, keys[o], best)
            best_at = jnp.where(more, I32(o), best_at)
        least, least_at = loads[0], I32(0)
        for p in range(1, planes):
            less = loads[p] < least
            least = jnp.where(less, loads[p], least)
            least_at = jnp.where(less, I32(p), least_at)
        loads = [jnp.where(least_at == p, loads[p] + best, loads[p]) for p in range(planes)]
        place = [jnp.where(best_at == o, least_at, place[o]) for o in range(owners)]
        keys = [jnp.where(best_at == o, F32(-1.0), keys[o]) for o in range(owners)]
    for c in range(clusters):
        plane_ref[c] = place[c // CL_OWN]
    top = None
    for p in range(planes):
        load = jnp.zeros_like(rows[0])
        for c in range(clusters):
            load = load + jnp.where(place[c // CL_OWN] == p, F32(1.0), F32(0.0)) * rows[c]
        top = load if top is None else jnp.maximum(top, load)
    top = jnp.max(top)
    tier = I32(0)
    for cap in caps[:-1]:
        tier = tier + jnp.where(top > cap, I32(1), I32(0))
    tier_ref[0] = tier


def pack_kernel(
    planes, cap, pieces, emb_ref, ids_ref, valid_ref, counts_ref, plane_ref, *refs
):
    out_refs, slot_ref, seen = refs[: len(pieces)], refs[len(pieces)], refs[len(pieces) + 1]
    clusters = counts_ref.shape[0]
    rows = emb_ref.shape[0]
    me = group_index()
    my_plane = lax.axis_index("own") // 2

    for p in range(planes):
        seen[p] = 0
    base = jnp.zeros((clusters, 1), F32)
    at = lax.broadcasted_iota(I32, (clusters, 1), 0)
    for c in range(clusters):
        p = plane_ref[c]
        first = (p ^ my_plane) * cap + seen[p]
        seen[p] = seen[p] + counts_ref[c, me]
        base = jnp.where(at == c, first.astype(F32), base)

    is_valid = lax.broadcasted_iota(I32, (1, rows), 1) < valid_ref[0]
    hit = (ids_ref[...] == lax.broadcasted_iota(I32, (clusters, rows), 0)) & is_valid
    upto = lax.broadcasted_iota(I32, (rows, rows), 0) <= lax.broadcasted_iota(I32, (rows, rows), 1)
    rank = jnp.dot(
        hit.astype(F32).astype(BF16), upto.astype(F32).astype(BF16), preferred_element_type=F32
    )
    slot = jnp.sum(jnp.where(hit, rank + (base - 1.0), 0.0), axis=0, keepdims=True)
    slot = jnp.where(is_valid, slot.astype(I32), -1)
    slot_ref[...] = slot

    wide = emb_ref[...].astype(F32)
    unit = (wide * lax.rsqrt(jnp.sum(wide * wide, axis=1, keepdims=True) + epsilon)).astype(BF16)
    for (o, start, size), out_ref in zip(pieces, out_refs):
        pick = slot == lax.broadcasted_iota(I32, (size, rows), 0) + (o * cap + start)
        out_ref[...] = jnp.dot(
            pick.astype(F32).astype(BF16), unit, preferred_element_type=F32
        ).astype(BF16)


def score_kernel(planes, cap, pieces, counts_ref, cnt_ref, plane_ref, *refs):
    n = len(pieces)
    key_refs = [refs[k * n : (k + 1) * n] for k in range(4)]
    out_refs = refs[4 * n : 4 * n + planes]
    keys, sems = refs[4 * n + planes :]
    clusters, lanes = counts_ref.shape
    queries = planes * cap
    my_plane = lax.axis_index("own") // 2
    side = lax.axis_index("own") % 2
    sub = lax.axis_index("sub")

    copies = []
    for k in range(4):
        for i, (o, start, size) in enumerate(pieces):
            copy = pltpu.make_async_copy(
                key_refs[k][i], keys.at[k, pl.ds(o * cap + start, size)], sems.at[k, i]
            )
            copy.start()
            copies.append((k, o, copy))

    def device(k, o):
        return ((my_plane ^ o) * 2 + (side ^ (k & 1))) * 2 + (sub ^ (k >> 1))

    counts = counts_ref[...]
    row_at = lax.broadcasted_iota(I32, (cap, lanes), 0)
    total = jnp.zeros((1, lanes), I32)
    label = jnp.zeros((cap, lanes), F32)
    slot_at = lax.broadcasted_iota(I32, (1, cap), 1)
    query_total = [I32(0)] * planes
    query_label = [jnp.zeros((1, cap), F32)] * planes
    for c in range(clusters):
        here = plane_ref[c] == my_plane
        total = total + jnp.where(here, counts[c : c + 1], 0)
        label = label + jnp.where(row_at >= total, 1.0, 0.0)
        for o in range(planes):
            query_total[o] = query_total[o] + jnp.where(here, cnt_ref[c, device(0, o)], 0)
            query_label[o] = query_label[o] + jnp.where(slot_at >= query_total[o], 1.0, 0.0)
    query_label = jnp.concatenate(query_label, axis=1)

    for k, o, copy in copies[:n]:
        copy.wait()
    lane_at = lax.broadcasted_iota(I32, (cap, lanes), 1)
    best = jnp.full((8, queries), -1.0, F32)
    for k in range(4):
        for o in range(planes):
            if k:
                for kk, oo, copy in copies:
                    if kk == k and oo == o:
                        copy.wait()
            scores = lax.dot_general(
                keys[k, o * cap : (o + 1) * cap],
                keys[0],
                (((1,), (1,)), ((), ())),
                preferred_element_type=F32,
            )
            key_label = jnp.sum(
                jnp.where(lane_at == device(k, o), label, 0.0), axis=1, keepdims=True
            )
            same = key_label == query_label
            if k == 0:
                same = same & (
                    lax.broadcasted_iota(I32, (cap, queries), 0) + o * cap
                    != lax.broadcasted_iota(I32, (cap, queries), 1)
                )
            masked = jnp.where(same, scores, -1.0)
            best = jnp.maximum(best, jnp.max(masked.reshape(cap // 8, 8, queries), axis=0))
    best = jnp.max(best, axis=0, keepdims=True)
    for o in range(planes):
        out_refs[o][...] = best[:, o * cap : (o + 1) * cap]


def place_kernel(planes, cap, slot_ref, valid_ref, *refs):
    back_refs, out_ref = refs[:planes], refs[planes]
    rows = slot_ref.shape[1]
    slot = slot_ref[...]
    part = jnp.zeros((1, rows), I32)
    for o in range(1, planes):
        part = part + jnp.where(slot >= o * cap, 1, 0)
    inner = slot - part * cap
    pick = (inner == lax.broadcasted_iota(I32, (cap, rows), 0)).astype(F32).astype(BF16)
    rest = jnp.concatenate([ref[...] for ref in back_refs], axis=0)
    found = jnp.zeros((planes, rows), F32)
    for _ in range(3):
        head = rest.astype(BF16)
        rest = rest - head.astype(F32)
        found = found + jnp.dot(head, pick, preferred_element_type=F32)
    chosen = part == lax.broadcasted_iota(I32, (planes, rows), 0)
    found = jnp.sum(jnp.where(chosen, found, 0.0), axis=0, keepdims=True)
    is_valid = lax.broadcasted_iota(I32, (1, rows), 1) < valid_ref[0]
    out_ref[...] = jnp.where(is_valid, found, 0.0)


def params():
    return pltpu.CompilerParams(vmem_limit_bytes=VMEM_LIMIT)


def across_planes(x, offset, owners):
    return lax.ppermute(x, "own", [(a, a ^ (2 * offset)) for a in range(owners)])


def across_sides(x, owners):
    return lax.ppermute(x, "own", [(a, a ^ 1) for a in range(owners)])


def across_subs(x):
    return lax.ppermute(x, "sub", [(0, 1), (1, 0)])


def exchange(cap, planes, owners, embeddings, ids, valid_counts, counts, plane_of):
    rows, width = embeddings.shape
    queries = planes * cap
    pieces = [(o, 0, cap) for o in range(planes)]

    packed = pl.pallas_call(
        lambda *r: pack_kernel(planes, cap, pieces, *r),
        out_shape=[jax.ShapeDtypeStruct((size, width), BF16) for _, _, size in pieces]
        + [jax.ShapeDtypeStruct((1, rows), I32)],
        in_specs=[vmem(), vmem(), smem(), smem(), smem()],
        out_specs=[vmem()] * (len(pieces) + 1),
        scratch_shapes=[pltpu.SMEM((planes,), I32)],
        compiler_params=params(),
        name="pack",
    )(embeddings, ids, valid_counts, counts, plane_of)
    blocks, slot = packed[:-1], packed[-1]

    own = [
        block if o == 0 else across_planes(block, o, owners)
        for (o, _, _), block in zip(pieces, blocks)
    ]
    other = [across_sides(block, owners) for block in own]
    own_peer = [across_subs(block) for block in own]
    other_peer = [across_subs(block) for block in other]

    best = pl.pallas_call(
        lambda *r: score_kernel(planes, cap, pieces, *r),
        out_shape=[jax.ShapeDtypeStruct((1, cap), F32)] * planes,
        in_specs=[vmem(), smem(), smem()] + [hbm()] * (4 * len(pieces)),
        out_specs=[vmem()] * planes,
        scratch_shapes=[
            pltpu.VMEM((4, queries, width), BF16),
            pltpu.SemaphoreType.DMA((4, len(pieces))),
        ],
        compiler_params=params(),
        name="score",
    )(counts, counts, plane_of, *own, *other, *own_peer, *other_peer)

    back = [best[0]] + [across_planes(best[o], o, owners) for o in range(1, planes)]
    return pl.pallas_call(
        lambda *r: place_kernel(planes, cap, *r),
        out_shape=jax.ShapeDtypeStruct((1, rows), F32),
        in_specs=[vmem(), smem()] + [vmem()] * planes,
        out_specs=vmem(),
        compiler_params=params(),
        name="place",
    )(slot, valid_counts, *back)


def shards(embeddings, cluster_ids, valid_counts):
    rows, width = embeddings.shape
    owners = lax.axis_size("own")
    planes = owners // 2
    clusters = CL_OWN * owners
    lanes = max(128, 2 * owners)
    ids = cluster_ids.reshape(1, rows)

    share = rows // planes
    caps = sorted({-(-share * k // 6 // 16) * 16 for k in (6, 8, 12)})

    counts = pl.pallas_call(
        count_kernel,
        out_shape=jax.ShapeDtypeStruct((clusters, lanes), I32),
        in_specs=[vmem(), smem()],
        out_specs=vmem(),
        name="count",
    )(ids, valid_counts)
    counts = lax.psum(counts, ("own", "sub"))
    plane_of, tier = pl.pallas_call(
        lambda *r: plan_kernel(planes, caps, *r),
        out_shape=[
            jax.ShapeDtypeStruct((clusters,), I32),
            jax.ShapeDtypeStruct((1,), I32),
        ],
        in_specs=[vmem()],
        out_specs=[smem(), smem()],
        name="plan",
    )(counts)

    def branch(cap):
        return lambda *a: exchange(cap, planes, owners, *a)

    nearest = lax.switch(
        tier[0],
        [branch(cap) for cap in caps],
        embeddings,
        ids,
        valid_counts,
        counts,
        plane_of,
    )
    return nearest.reshape(rows)


def solution(mesh):
    in_specs = (
        P(("groups", "own", "sub"), None),
        P(("groups", "own", "sub")),
        P(("groups", "own", "sub")),
    )
    out_specs = P(("groups", "own", "sub"))
    return jax.shard_map(shards, mesh=mesh, in_specs=in_specs, out_specs=out_specs, check_vma=False)
```

```python
import jax
import jax.numpy as jnp
from jax import lax
from jax.experimental import pallas as pl
from jax.experimental.pallas import tpu as pltpu
from jax.sharding import PartitionSpec as P

CL_OWN = 2
epsilon = 1e-06

F32 = jnp.float32
BF16 = jnp.bfloat16
I32 = jnp.int32


def vmem():
    return pl.BlockSpec(memory_space=pltpu.VMEM)


def smem():
    return pl.BlockSpec(memory_space=pltpu.SMEM)


def group_index():
    return lax.axis_index("own") * 2 + lax.axis_index("sub")


def hits(clusters, marked):
    return marked == lax.broadcasted_iota(I32, (clusters, marked.shape[1]), 0)


def count_kernel(ids_ref, valid_ref, out_ref, marked_ref):
    clusters, lanes = out_ref.shape
    rows = ids_ref.shape[0]
    is_valid = lax.broadcasted_iota(I32, (1, rows), 1) < valid_ref[...].reshape(1, 1)
    marked = jnp.where(is_valid, ids_ref[...].reshape(1, rows), -1)
    marked_ref[...] = marked
    total = jnp.sum(hits(clusters, marked).astype(F32), axis=1, keepdims=True).astype(I32)
    mine = lax.broadcasted_iota(I32, (clusters, lanes), 1) == group_index()
    out_ref[...] = jnp.where(mine, total, 0)


def spread(keys, planes):
    keys = list(keys)
    loads = [F32(0.0)] * planes
    place = [I32(0)] * len(keys)
    for _ in range(len(keys)):
        ranked = [(key, I32(i)) for i, key in enumerate(keys)]
        while len(ranked) > 1:
            ranked = [
                (jnp.maximum(a, b), jnp.where(b > a, bi, ai))
                for (a, ai), (b, bi) in zip(ranked[::2], ranked[1::2])
            ]
        best, best_at = ranked[0]
        ranked = [(load, I32(p)) for p, load in enumerate(loads)]
        while len(ranked) > 1:
            ranked = [
                (jnp.minimum(a, b), jnp.where(b < a, bi, ai))
                for (a, ai), (b, bi) in zip(ranked[::2], ranked[1::2])
            ]
        least_at = ranked[0][1]
        loads = [jnp.where(least_at == p, load + best, load) for p, load in enumerate(loads)]
        place = [jnp.where(best_at == i, least_at, at) for i, at in enumerate(place)]
        keys = [jnp.where(best_at == i, F32(-1.0), key) for i, key in enumerate(keys)]
    return place


def top_load(place, rows, planes):
    top = jnp.zeros_like(rows[0])
    for p in range(planes):
        load = jnp.zeros_like(rows[0])
        for at, row in zip(place, rows):
            load = load + jnp.where(at == p, F32(1.0), F32(0.0)) * row
        top = jnp.maximum(top, load)
    return jnp.max(top)


def plan_kernel(planes, caps, counts_ref, plane_ref, tier_ref):
    clusters = counts_ref.shape[0]
    counts = counts_ref[...].astype(F32)
    rows = [counts[c : c + 1] for c in range(clusters)]
    pairs = [rows[c] + rows[c + 1] for c in range(0, clusters, CL_OWN)]
    place = spread([jnp.max(pair) for pair in pairs], planes)
    top = top_load(place, pairs, planes)
    place = [place[c // CL_OWN] for c in range(clusters)]
    if clusters <= 16:
        finer = spread([jnp.sum(row) for row in rows], planes)
        finer_top = top_load(finer, rows, planes)
        better = finer_top < top
        top = jnp.minimum(top, finer_top)
        place = [jnp.where(better, b, a) for a, b in zip(place, finer)]
    for c in range(clusters):
        plane_ref[c] = place[c]
    tier = I32(0)
    for cap in caps[:-1]:
        tier = tier + jnp.where(top > cap, I32(1), I32(0))
    tier_ref[0] = tier


def unit_kernel(emb_ref, marked_ref, counts_ref, unit_ref, rank_ref):
    clusters = counts_ref.shape[0]
    rows = emb_ref.shape[0]
    hit = hits(clusters, marked_ref[...])
    upto = lax.broadcasted_iota(I32, (rows, rows), 0) <= lax.broadcasted_iota(I32, (rows, rows), 1)
    rank_ref[...] = jnp.where(
        hit,
        jnp.dot(
            hit.astype(F32).astype(BF16),
            upto.astype(F32).astype(BF16),
            preferred_element_type=F32,
        ),
        0.0,
    )
    wide = emb_ref[...].astype(F32)
    unit_ref[...] = (
        wide * lax.rsqrt(jnp.sum(wide * wide, axis=1, keepdims=True) + epsilon)
    ).astype(BF16)


def slot_kernel(planes, cap, rank_ref, counts_ref, plane_ref, seen):
    clusters, rows = rank_ref.shape
    me = group_index()
    my_plane = lax.axis_index("own") // 2
    for p in range(planes):
        seen[p] = 0
    base = jnp.zeros((clusters, 1), F32)
    at = lax.broadcasted_iota(I32, (clusters, 1), 0)
    for c in range(clusters):
        p = plane_ref[c]
        first = (p ^ my_plane) * cap + seen[p]
        seen[p] = seen[p] + counts_ref[c, me]
        base = jnp.where(at == c, first.astype(F32), base)
    rank = rank_ref[...]
    slot = jnp.sum(jnp.where(rank > 0.0, rank + base, 0.0), axis=0, keepdims=True)
    return slot.astype(I32) - 1


def pick_rows(pieces, slot, unit_ref, out_refs):
    unit = unit_ref[...]
    for (_, _, size, begin), out_ref in zip(pieces, out_refs):
        at = lax.broadcasted_iota(I32, (size, slot.shape[1]), 0) + begin
        pick = (slot == at).astype(F32).astype(BF16)
        out_ref[...] = jnp.dot(pick, unit, preferred_element_type=F32).astype(BF16)


def pack_kernel(planes, cap, pieces, unit_ref, rank_ref, counts_ref, plane_ref, *refs):
    *out_refs, slot_ref, seen = refs
    slot = slot_kernel(planes, cap, rank_ref, counts_ref, plane_ref, seen)
    slot_ref[...] = slot
    pick_rows(pieces, slot, unit_ref, out_refs)


def repack_kernel(pieces, unit_ref, slot_ref, *out_refs):
    pick_rows(pieces, slot_ref[...], unit_ref, out_refs)


def source(k, o):
    plane, side = lax.axis_index("own") // 2, lax.axis_index("own") % 2
    return ((plane ^ o) * 2 + (side ^ (k & 1))) * 2 + (lax.axis_index("sub") ^ (k >> 1))


def labels(planes, cap, counts_ref, cnt_ref, plane_ref):
    clusters, lanes = counts_ref.shape
    my_plane = lax.axis_index("own") // 2
    counts = counts_ref[...]
    row_at = lax.broadcasted_iota(I32, (cap, lanes), 0)
    slot_at = lax.broadcasted_iota(I32, (1, cap), 1)
    key_total = jnp.zeros((1, lanes), I32)
    key_label = jnp.zeros((cap, lanes), F32)
    devices = [source(k, o) for k in (0, 2) for o in range(planes)]
    query_total = [I32(0)] * len(devices)
    query_label = [jnp.zeros((1, cap), F32)] * len(devices)
    for c in range(clusters):
        here = plane_ref[c] == my_plane
        key_total = key_total + jnp.where(here, counts[c : c + 1], 0)
        key_label = key_label + jnp.where(row_at >= key_total, 1.0, 0.0)
        for i, device in enumerate(devices):
            query_total[i] = query_total[i] + jnp.where(here, cnt_ref[c, device], 0)
            query_label[i] = query_label[i] + jnp.where(slot_at >= query_total[i], 1.0, 0.0)
    return key_label, [
        jnp.concatenate(query_label[k * planes : (k + 1) * planes], axis=1) for k in range(2)
    ]


def column(key_label, k, piece):
    o, start, size, _ = piece
    part = key_label[start : start + size]
    at = lax.broadcasted_iota(I32, part.shape, 1)
    return jnp.sum(jnp.where(at == source(k, o), part, 0.0), axis=1, keepdims=True)


def fold(best, scores, key_label, query_label, distance):
    same = key_label == query_label
    if distance is not None:
        size, width = scores.shape
        same = same & (
            lax.broadcasted_iota(I32, (size, width), 0) + distance
            != lax.broadcasted_iota(I32, (size, width), 1)
        )
    masked = jnp.where(same, scores, -1.0)
    size, width = scores.shape
    return jnp.maximum(best, jnp.max(masked.reshape(size // 8, 8, width), axis=0))


def score(a, b):
    return lax.dot_general(a, b, (((1,), (1,)), ((), ())), preferred_element_type=F32)


def gather(refs):
    return jnp.concatenate([ref[...] for ref in refs], axis=0)


def fold_pieces(best, scores, key_label, k, pieces, query_label, meets_itself):
    start = 0
    for piece in pieces:
        size = piece[2]
        best = fold(
            best,
            scores[start : start + size],
            column(key_label, k, piece),
            query_label,
            piece[3] if meets_itself else None,
        )
        start += size
    return best


def early_kernel(planes, cap, pieces, counts_ref, cnt_ref, plane_ref, *refs):
    n = len(pieces)
    own, other, peer = (refs[k * n : (k + 1) * n] for k in range(3))
    out_ref = refs[3 * n]
    key_label, query_label = labels(planes, cap, counts_ref, cnt_ref, plane_ref)
    rows = gather(own)
    width = rows.shape[0]
    query_label = jnp.concatenate([label[:, :width] for label in query_label], axis=1)
    queries = jnp.concatenate([rows, gather(peer)], axis=0)
    best = jnp.full((8, 2 * width), -1.0, F32)
    best = fold_pieces(best, score(rows, queries), key_label, 0, pieces, query_label, True)
    scores = score(gather(other), queries)
    best = fold_pieces(best, scores, key_label, 1, pieces, query_label, False)
    out_ref[...] = jnp.max(best, axis=0, keepdims=True)


def middle_kernel(planes, cap, pieces, first, counts_ref, cnt_ref, plane_ref, early_ref, *refs):
    n = len(pieces)
    own, other, peer = refs[:n], refs[n : 2 * n - 1], refs[2 * n - 1 : 3 * n - 1]
    mine_ref, theirs_ref = refs[3 * n - 1 :]
    key_label, query_label = labels(planes, cap, counts_ref, cnt_ref, plane_ref)
    edge = pieces[first][3]
    rows, others, peers = gather(own), gather(other), gather(peer)
    width = rows.shape[0]
    late_label = jnp.concatenate([label[:, edge:] for label in query_label], axis=1)
    all_label = jnp.concatenate(query_label, axis=1)
    queries = jnp.concatenate([rows[edge:], peers[edge:]], axis=0)
    late = jnp.full((8, 2 * (width - edge)), -1.0, F32)
    for k, held in enumerate((rows, others)):
        scores = score(held[:edge], queries)
        late = fold_pieces(late, scores, key_label, k, pieces[:first], late_label, False)
    late = jnp.max(late, axis=0, keepdims=True)
    queries = jnp.concatenate([rows, peers], axis=0)
    best = jnp.full((8, 2 * width), -1.0, F32)
    for k, held in enumerate((rows, others)):
        scores = score(held[edge:], queries)
        best = fold_pieces(
            best, scores, key_label, k, pieces[first : n - k], all_label, k == 0
        )
    best = jnp.max(best, axis=0, keepdims=True)
    early = early_ref[...]
    for k, out_ref in enumerate((mine_ref, theirs_ref)):
        out_ref[:, :edge] = jnp.maximum(
            best[:, k * width : k * width + edge], early[:, k * edge : (k + 1) * edge]
        )
        out_ref[:, edge:] = jnp.maximum(
            best[:, k * width + edge : (k + 1) * width],
            late[:, k * (width - edge) : (k + 1) * (width - edge)],
        )


def last_kernel(planes, cap, pieces, counts_ref, cnt_ref, plane_ref, mine_ref, theirs_ref, *refs):
    n = len(pieces)
    own, keys, out_refs = refs[:n], refs[n : n + 2], refs[n + 2 :]
    key_label, query_label = labels(planes, cap, counts_ref, cnt_ref, plane_ref)
    rows = gather(own)
    best = jnp.full((8, rows.shape[0]), -1.0, F32)
    scores = score(gather(keys), rows)
    size = pieces[-1][2]
    for i, k in enumerate((1, 3)):
        part = scores[i * size : (i + 1) * size]
        best = fold_pieces(best, part, key_label, k, pieces[-1:], query_label[0], False)
    best = jnp.max(best, axis=0, keepdims=True)
    best = jnp.maximum(best, jnp.maximum(mine_ref[...], theirs_ref[...]))
    for o in range(planes):
        out_refs[o][...] = best[:, o * cap : (o + 1) * cap]


def place_kernel(planes, cap, slot_ref, *refs):
    back_refs, out_ref = refs[:planes], refs[planes]
    rows = slot_ref.shape[1]
    slot = slot_ref[...]
    part = jnp.zeros((1, rows), I32)
    for o in range(1, planes):
        part = part + jnp.where(slot >= o * cap, 1, 0)
    inner = slot - part * cap
    pick = (inner == lax.broadcasted_iota(I32, (cap, rows), 0)).astype(F32).astype(BF16)
    rest = jnp.concatenate([ref[...] for ref in back_refs], axis=0)
    found = jnp.zeros((planes, rows), F32)
    for _ in range(3):
        head = rest.astype(BF16)
        rest = rest - head.astype(F32)
        found = found + jnp.dot(head, pick, preferred_element_type=F32)
    chosen = part == lax.broadcasted_iota(I32, (planes, rows), 0)
    found = jnp.sum(jnp.where(chosen, found, 0.0), axis=0, keepdims=True)
    out_ref[...] = jnp.where(slot >= 0, found, 0.0).reshape(rows)


def params(limit=24):
    return pltpu.CompilerParams(vmem_limit_bytes=limit * 1024 * 1024)


def cost(rows, columns, depth):
    return pl.CostEstimate(
        flops=2 * rows * columns * depth,
        bytes_accessed=2 * (rows + columns) * depth,
        transcendentals=0,
    )


def after(x, *y):
    return lax.optimization_barrier((x, *y))[0] if y else x


def across_planes(x, offset, owners):
    return lax.ppermute(x, "own", [(a, a ^ (2 * offset)) for a in range(owners)])


def across_sides(x, owners):
    return lax.ppermute(x, "own", [(a, a ^ 1) for a in range(owners)])


def across_subs(x):
    return lax.ppermute(x, "sub", [(0, 1), (1, 0)])


def exchange(cap, planes, owners, unit, rank, counts, plane_of):
    rows, width = unit.shape
    tail = -(-cap // 48) * 16
    pieces = [(o, 0, cap, o * cap) for o in range(planes - 1)]
    last = planes - 1
    pieces += [
        (last, 0, cap - tail, last * cap),
        (last, cap - tail, tail, (last + 1) * cap - tail),
    ]

    n, half = len(pieces), planes // 2

    now, later = range(1, half + 1), [0, *range(half + 1, n)]
    *out, slot = pl.pallas_call(
        lambda *r: pack_kernel(planes, cap, [pieces[i] for i in now], *r),
        out_shape=[jax.ShapeDtypeStruct((pieces[i][2], width), BF16) for i in now]
        + [jax.ShapeDtypeStruct((1, rows), I32)],
        in_specs=[vmem(), vmem(), smem(), smem()],
        out_specs=[vmem()] * (len(now) + 1),
        scratch_shapes=[pltpu.SMEM((planes,), I32)],
        compiler_params=params(),
        name="pack",
    )(unit, rank, counts, plane_of)
    blocks = dict(zip(now, out))
    out = pl.pallas_call(
        lambda *r: repack_kernel([pieces[i] for i in later], *r),
        out_shape=[jax.ShapeDtypeStruct((pieces[i][2], width), BF16) for i in later],
        in_specs=[vmem(), vmem()],
        out_specs=[vmem()] * len(later),
        compiler_params=params(),
        cost_estimate=cost(sum(pieces[i][2] for i in later), rows, width),
        name="repack",
    )(unit, slot)
    blocks |= dict(zip(later, out))
    own, other, peer = ([None] * n for _ in range(3))
    own[0] = blocks[0]
    for i in range(1, n):
        block = blocks[i] if i <= half else after(blocks[i], own[i - 1])
        own[i] = across_planes(block, pieces[i][0], owners)
    for i in range(n - 1):
        other[i] = across_sides(after(own[i], other[0]) if i == 1 else own[i], owners)
    for i in range(n):
        gate = [own[half], other[1]] if i <= half else other[half:i]
        peer[i] = across_subs(after(own[i], *gate))

    first = last
    edge = last * cap
    meta = (counts, counts, plane_of)
    meta_specs = [vmem(), smem(), smem()]
    early = pl.pallas_call(
        lambda *r: early_kernel(planes, cap, pieces[:first], *r),
        out_shape=jax.ShapeDtypeStruct((1, 2 * edge), F32),
        in_specs=meta_specs + [vmem()] * (3 * first),
        out_specs=vmem(),
        compiler_params=params(),
        cost_estimate=cost(2 * edge, 2 * edge, width),
        name="early",
    )(*meta, *own[:first], *other[:first], *peer[:first])
    other[-1] = across_sides(after(own[-1], early), owners)
    mine, theirs = pl.pallas_call(
        lambda *r: middle_kernel(planes, cap, pieces, first, *r),
        out_shape=[jax.ShapeDtypeStruct((1, planes * cap), F32)] * 2,
        in_specs=meta_specs + [vmem()] * (3 * n),
        out_specs=[vmem()] * 2,
        compiler_params=params(),
        cost_estimate=cost(2 * edge, 4 * cap, width),
        name="middle",
    )(*meta, early, *own, *other[:-1], *peer)
    best = pl.pallas_call(
        lambda *r: last_kernel(planes, cap, pieces, *r),
        out_shape=[jax.ShapeDtypeStruct((1, cap), F32)] * planes,
        in_specs=meta_specs + [vmem()] * (n + 4),
        out_specs=[vmem()] * planes,
        compiler_params=params(),
        name="last",
    )(*meta, mine, across_subs(theirs), *own, other[-1], across_subs(after(other[-1], theirs)))

    back = [best[0]] + [across_planes(best[o], o, owners) for o in range(1, planes)]
    return pl.pallas_call(
        lambda *r: place_kernel(planes, cap, *r),
        out_shape=jax.ShapeDtypeStruct((rows,), F32),
        in_specs=[vmem()] * (planes + 1),
        out_specs=vmem(),
        compiler_params=params(8),
        name="place",
    )(slot, *back)


def shards(embeddings, cluster_ids, valid_counts):
    rows, width = embeddings.shape
    owners = lax.axis_size("own")
    planes = owners // 2
    clusters = CL_OWN * owners
    lanes = max(128, 2 * owners)

    share = rows // planes
    caps = sorted({-(-share * k // 12 // 16) * 16 for k in (12, 15, 24)})

    counts, marked = pl.pallas_call(
        count_kernel,
        out_shape=[
            jax.ShapeDtypeStruct((clusters, lanes), I32),
            jax.ShapeDtypeStruct((1, rows), I32),
        ],
        in_specs=[vmem(), vmem()],
        out_specs=[vmem(), vmem()],
        compiler_params=params(2),
        name="count",
    )(cluster_ids, valid_counts)
    counts = lax.psum(counts, ("own", "sub"))
    plane_of, tier = pl.pallas_call(
        lambda *r: plan_kernel(planes, caps, *r),
        out_shape=[
            jax.ShapeDtypeStruct((clusters,), I32),
            jax.ShapeDtypeStruct((1,), I32),
        ],
        in_specs=[vmem()],
        out_specs=[smem(), smem()],
        compiler_params=params(2),
        name="plan",
    )(counts)

    unit, rank = pl.pallas_call(
        unit_kernel,
        out_shape=[
            jax.ShapeDtypeStruct((rows, width), BF16),
            jax.ShapeDtypeStruct((clusters, rows), F32),
        ],
        in_specs=[vmem()] * 3,
        out_specs=[vmem()] * 2,
        compiler_params=params(16),
        name="unit",
    )(embeddings, marked, counts)

    def branch(cap):
        return lambda *a: exchange(cap, planes, owners, *a)

    nearest = lax.switch(
        tier[0],
        [branch(cap) for cap in caps],
        unit,
        rank,
        counts,
        plane_of,
    )
    return nearest


def solution(mesh):
    in_specs = (
        P(("groups", "own", "sub"), None),
        P(("groups", "own", "sub")),
        P(("groups", "own", "sub")),
    )
    out_specs = P(("groups", "own", "sub"))
    return jax.shard_map(shards, mesh=mesh, in_specs=in_specs, out_specs=out_specs, check_vma=False)
```

```python
import jax
import jax.numpy as jnp
from jax import lax
from jax.experimental import pallas as pl
from jax.experimental.pallas import tpu as pltpu
from jax.sharding import PartitionSpec as P

CL_OWN = 2
epsilon = 1e-06

F32 = jnp.float32
BF16 = jnp.bfloat16
I32 = jnp.int32


def vmem():
    return pl.BlockSpec(memory_space=pltpu.VMEM)


def smem():
    return pl.BlockSpec(memory_space=pltpu.SMEM)


def hbm():
    return pl.BlockSpec(memory_space=pltpu.HBM)


def group_index():
    return lax.axis_index("own") * 2 + lax.axis_index("sub")


def hits(clusters, marked):
    return marked == lax.broadcasted_iota(I32, (clusters, marked.shape[1]), 0)


def count_kernel(ids_ref, valid_ref, out_ref, marked_ref):
    clusters, lanes = out_ref.shape
    rows = ids_ref.shape[0]
    is_valid = lax.broadcasted_iota(I32, (1, rows), 1) < valid_ref[...].reshape(1, 1)
    marked = jnp.where(is_valid, ids_ref[...].reshape(1, rows), -1)
    marked_ref[...] = marked
    total = jnp.sum(hits(clusters, marked).astype(F32), axis=1, keepdims=True).astype(I32)
    mine = lax.broadcasted_iota(I32, (clusters, lanes), 1) == group_index()
    out_ref[...] = jnp.where(mine, total, 0)


def spread(keys, planes):
    keys = list(keys)
    loads = [F32(0.0)] * planes
    place = [I32(0)] * len(keys)
    for _ in range(len(keys)):
        ranked = [(key, I32(i)) for i, key in enumerate(keys)]
        while len(ranked) > 1:
            ranked = [
                (jnp.maximum(a, b), jnp.where(b > a, bi, ai))
                for (a, ai), (b, bi) in zip(ranked[::2], ranked[1::2])
            ]
        best, best_at = ranked[0]
        ranked = [(load, I32(p)) for p, load in enumerate(loads)]
        while len(ranked) > 1:
            ranked = [
                (jnp.minimum(a, b), jnp.where(b < a, bi, ai))
                for (a, ai), (b, bi) in zip(ranked[::2], ranked[1::2])
            ]
        least_at = ranked[0][1]
        loads = [jnp.where(least_at == p, load + best, load) for p, load in enumerate(loads)]
        place = [jnp.where(best_at == i, least_at, at) for i, at in enumerate(place)]
        keys = [jnp.where(best_at == i, F32(-1.0), key) for i, key in enumerate(keys)]
    return place


def top_load(place, rows, planes):
    top = jnp.zeros_like(rows[0])
    for p in range(planes):
        load = jnp.zeros_like(rows[0])
        for at, row in zip(place, rows):
            load = load + jnp.where(at == p, F32(1.0), F32(0.0)) * row
        top = jnp.maximum(top, load)
    return jnp.max(top)


def plan(planes, caps, counts_ref, plane_ref, tier_ref):
    clusters = counts_ref.shape[0]
    counts = counts_ref[...].astype(F32)
    rows = [counts[c : c + 1] for c in range(clusters)]
    pairs = [rows[c] + rows[c + 1] for c in range(0, clusters, CL_OWN)]
    place = spread([jnp.max(pair) for pair in pairs], planes)
    top = top_load(place, pairs, planes)
    place = [place[c // CL_OWN] for c in range(clusters)]
    if clusters <= 16:
        finer = spread([jnp.sum(row) for row in rows], planes)
        finer_top = top_load(finer, rows, planes)
        better = finer_top < top
        top = jnp.minimum(top, finer_top)
        place = [jnp.where(better, b, a) for a, b in zip(place, finer)]
    for c in range(clusters):
        plane_ref[c] = place[c]
    tier = I32(0)
    for cap in caps[:-1]:
        tier = tier + jnp.where(top > cap, I32(1), I32(0))
    tier_ref[0] = tier


def unit_kernel(
    planes, caps, emb_ref, marked_ref, counts_ref, unit_ref, rank_ref, plane_ref, tier_ref, wide, sem
):
    copy = pltpu.make_async_copy(emb_ref, wide, sem)
    copy.start()
    clusters = counts_ref.shape[0]
    rows = emb_ref.shape[0]
    hit = hits(clusters, marked_ref[...])
    upto = lax.broadcasted_iota(I32, (rows, rows), 0) <= lax.broadcasted_iota(I32, (rows, rows), 1)
    rank_ref[...] = jnp.where(
        hit,
        jnp.dot(
            hit.astype(F32).astype(BF16),
            upto.astype(F32).astype(BF16),
            preferred_element_type=F32,
        ),
        0.0,
    )
    plan(planes, caps, counts_ref, plane_ref, tier_ref)
    copy.wait()
    x = wide[...].astype(F32)
    unit_ref[...] = (
        x * lax.rsqrt(jnp.sum(x * x, axis=1, keepdims=True) + epsilon)
    ).astype(BF16)


def slot_kernel(order, cap, rank_ref, counts_ref, plane_ref, seen):
    clusters, rows = rank_ref.shape
    me = group_index()
    my_plane = lax.axis_index("own") // 2
    for p in range(len(order)):
        seen[p] = 0
    base = jnp.zeros((clusters, 1), F32)
    at = lax.broadcasted_iota(I32, (clusters, 1), 0)
    for c in range(clusters):
        p = plane_ref[c]
        block = I32(0)
        for b, o in enumerate(order):
            block = jnp.where((p ^ my_plane) == o, I32(b), block)
        first = block * cap + seen[p]
        seen[p] = seen[p] + counts_ref[c, me]
        base = jnp.where(at == c, first.astype(F32), base)
    rank = rank_ref[...]
    slot = jnp.sum(jnp.where(rank > 0.0, rank + base, 0.0), axis=0, keepdims=True)
    return slot.astype(I32) - 1


def pick_rows(pieces, slot, unit_ref, out_refs):
    unit = unit_ref[...]
    for (_, _, size, begin), out_ref in zip(pieces, out_refs):
        at = lax.broadcasted_iota(I32, (size, slot.shape[1]), 0) + begin
        pick = (slot == at).astype(F32).astype(BF16)
        out_ref[...] = jnp.dot(pick, unit, preferred_element_type=F32).astype(BF16)


def pack_kernel(order, cap, pieces, unit_ref, rank_ref, counts_ref, plane_ref, *refs):
    *out_refs, slot_ref, seen = refs
    slot = slot_kernel(order, cap, rank_ref, counts_ref, plane_ref, seen)
    slot_ref[...] = slot
    pick_rows(pieces, slot, unit_ref, out_refs)


def repack_kernel(pieces, unit_ref, slot_ref, *out_refs):
    pick_rows(pieces, slot_ref[...], unit_ref, out_refs)


def source(k, o):
    plane, side = lax.axis_index("own") // 2, lax.axis_index("own") % 2
    return ((plane ^ o) * 2 + (side ^ (k & 1))) * 2 + (lax.axis_index("sub") ^ (k >> 1))


def label_kernel(order, cap, counts_ref, cnt_ref, plane_ref, keys_ref, queries_ref):
    clusters, lanes = counts_ref.shape
    my_plane = lax.axis_index("own") // 2
    counts = counts_ref[...]
    row_at = lax.broadcasted_iota(I32, (cap, lanes), 0)
    lane_at = lax.broadcasted_iota(I32, (cap, lanes), 1)
    slot_at = lax.broadcasted_iota(I32, (1, cap), 1)
    key_total = jnp.zeros((1, lanes), I32)
    key_label = jnp.zeros((cap, lanes), F32)
    devices = [source(k, o) for k in (0, 2) for o in order]
    query_total = [I32(0)] * len(devices)
    query_label = [jnp.zeros((1, cap), F32)] * len(devices)
    for c in range(clusters):
        here = plane_ref[c] == my_plane
        key_total = key_total + jnp.where(here, counts[c : c + 1], 0)
        key_label = key_label + jnp.where(row_at >= key_total, 1.0, 0.0)
        for i, device in enumerate(devices):
            query_total[i] = query_total[i] + jnp.where(here, cnt_ref[c, device], 0)
            query_label[i] = query_label[i] + jnp.where(slot_at >= query_total[i], 1.0, 0.0)
    queries_ref[...] = jnp.concatenate(query_label, axis=1)
    columns = jnp.zeros((cap, lanes), F32)
    for k in range(4):
        for b, o in enumerate(order):
            one = jnp.where(lane_at == source(k, o), key_label, 0.0)
            one = jnp.sum(one, axis=1, keepdims=True)
            columns = jnp.where(lane_at == k * len(order) + b, one, columns)
    keys_ref[...] = columns


def fold(best, scores, key_label, query_label, distance):
    same = key_label == query_label
    if distance is not None:
        size, width = scores.shape
        same = same & (
            lax.broadcasted_iota(I32, (size, width), 0) + distance
            != lax.broadcasted_iota(I32, (size, width), 1)
        )
    masked = jnp.where(same, scores, -1.0)
    size, width = scores.shape
    return jnp.maximum(best, jnp.max(masked.reshape(size // 8, 8, width), axis=0))


def score(a, b):
    return lax.dot_general(a, b, (((1,), (1,)), ((), ())), preferred_element_type=F32)


def gather(refs):
    return jnp.concatenate([ref[...] for ref in refs], axis=0)


def fold_pieces(best, scores, keys_ref, planes, parts, query_label):
    at = 0
    for (b, start, size, begin), k, among in parts:
        best = fold(
            best,
            scores[at : at + size],
            keys_ref[start : start + size, k * planes + b : k * planes + b + 1],
            query_label,
            begin if among else None,
        )
        at += size
    return jnp.max(best, axis=0, keepdims=True)


def early_kernel(planes, pieces, e, f, keys_ref, queries_ref, *refs):
    own, other, peer, out_ref = refs[:e], refs[e : e + f], refs[e + f : 2 * e + f], refs[-1]
    rows = gather(own)
    edge, total = rows.shape[0], queries_ref.shape[1] // 2
    label = queries_ref[...]
    label = jnp.concatenate([label[:, :edge], label[:, total : total + edge]], axis=1)
    queries = jnp.concatenate([rows, gather(peer)], axis=0)
    scores = score(jnp.concatenate([rows, gather(other)], axis=0), queries)
    parts = [(piece, 0, True) for piece in pieces[:e]] + [(piece, 1, False) for piece in pieces[:f]]
    best = jnp.full((8, 2 * edge), -1.0, F32)
    out_ref[...] = fold_pieces(best, scores, keys_ref, planes, parts, label)


def middle_kernel(planes, pieces, e, f, keys_ref, queries_ref, early_ref, *refs):
    n = len(pieces)
    own, other, peer = refs[:n], refs[n : 2 * n - 1], refs[2 * n - 1 : 3 * n - 1]
    mine_ref, theirs_ref = refs[3 * n - 1 :]
    rows, peers = gather(own), gather(peer)
    width, edge = rows.shape[0], pieces[e][3]
    label = queries_ref[...]
    late_label = jnp.concatenate([label[:, edge:width], label[:, width + edge :]], axis=1)
    queries = jnp.concatenate([rows[edge:], peers[edge:]], axis=0)
    scores = score(jnp.concatenate([rows[:edge], gather(other[:f])], axis=0), queries)
    parts = [(piece, 0, False) for piece in pieces[:e]]
    parts += [(piece, 1, False) for piece in pieces[:f]]
    late = jnp.full((8, 2 * (width - edge)), -1.0, F32)
    late = fold_pieces(late, scores, keys_ref, planes, parts, late_label)

    queries = jnp.concatenate([rows, peers], axis=0)
    held = jnp.concatenate([rows[edge:], *[ref[...] for ref in other[f:]]], axis=0)
    parts = [(piece, 0, True) for piece in pieces[e:]]
    parts += [(piece, 1, False) for piece in pieces[f : n - 1]]
    best = jnp.full((8, 2 * width), -1.0, F32)
    best = fold_pieces(best, score(held, queries), keys_ref, planes, parts, label)
    early = early_ref[...]
    for k, out_ref in enumerate((mine_ref, theirs_ref)):
        out_ref[:, :edge] = jnp.maximum(
            best[:, k * width : k * width + edge], early[:, k * edge : (k + 1) * edge]
        )
        out_ref[:, edge:] = jnp.maximum(
            best[:, k * width + edge : (k + 1) * width],
            late[:, k * (width - edge) : (k + 1) * (width - edge)],
        )


def last_kernel(planes, cap, pieces, keys_ref, queries_ref, mine_ref, theirs_ref, *refs):
    n = len(pieces)
    own, keys, out_refs = refs[:n], refs[n : n + 2], refs[n + 2 :]
    rows = gather(own)
    width = rows.shape[0]
    best = jnp.full((8, width), -1.0, F32)
    parts = [(pieces[-1], 1, False), (pieces[-1], 3, False)]
    label = queries_ref[:, :width]
    best = fold_pieces(best, score(gather(keys), rows), keys_ref, planes, parts, label)
    best = jnp.maximum(best, jnp.maximum(mine_ref[...], theirs_ref[...]))
    for b in range(planes):
        out_refs[b][...] = best[:, b * cap : (b + 1) * cap]


def place_kernel(planes, cap, slot_ref, *refs):
    back_refs, out_ref = refs[:planes], refs[planes]
    rows = slot_ref.shape[1]
    slot = slot_ref[...]
    part = jnp.zeros((1, rows), I32)
    for o in range(1, planes):
        part = part + jnp.where(slot >= o * cap, 1, 0)
    inner = slot - part * cap
    pick = (inner == lax.broadcasted_iota(I32, (cap, rows), 0)).astype(F32).astype(BF16)
    rest = jnp.concatenate([ref[...] for ref in back_refs], axis=0)
    found = jnp.zeros((planes, rows), F32)
    for _ in range(3):
        head = rest.astype(BF16)
        rest = rest - head.astype(F32)
        found = found + jnp.dot(head, pick, preferred_element_type=F32)
    chosen = part == lax.broadcasted_iota(I32, (planes, rows), 0)
    found = jnp.sum(jnp.where(chosen, found, 0.0), axis=0, keepdims=True)
    out_ref[...] = jnp.where(slot >= 0, found, 0.0).reshape(rows)


def params(limit=24):
    return pltpu.CompilerParams(vmem_limit_bytes=limit * 1024 * 1024)


def cost(rows, columns, depth):
    return pl.CostEstimate(
        flops=2 * rows * columns * depth,
        bytes_accessed=2 * (rows + columns) * depth,
        transcendentals=0,
    )


def after(x, *y):
    return lax.optimization_barrier((x, *y))[0] if y else x


def across_planes(x, offset, owners, side=0):
    return lax.ppermute(x, "own", [(a, a ^ (2 * offset + side)) for a in range(owners)])


def across_sides(x, owners):
    return lax.ppermute(x, "own", [(a, a ^ 1) for a in range(owners)])


def across_subs(x):
    return lax.ppermute(x, "sub", [(0, 1), (1, 0)])


def exchange(cap, planes, owners, unit, rank, counts, plane_of):
    rows, width = unit.shape
    tail = -(-cap // 48) * 16
    half, last = planes // 2, planes - 1
    order = [0, half, *range(1, half), *range(half + 1, planes)]
    pieces = [(b, 0, cap, b * cap) for b in range(last)]
    pieces += [
        (last, 0, cap - tail, last * cap),
        (last, cap - tail, tail, (last + 1) * cap - tail),
    ]
    n = len(pieces)

    now, later = [1], [i for i in range(n) if i != 1]
    *out, slot = pl.pallas_call(
        lambda *r: pack_kernel(order, cap, [pieces[i] for i in now], *r),
        out_shape=[jax.ShapeDtypeStruct((pieces[i][2], width), BF16) for i in now]
        + [jax.ShapeDtypeStruct((1, rows), I32)],
        in_specs=[vmem(), vmem(), smem(), smem()],
        out_specs=[vmem()] * (len(now) + 1),
        scratch_shapes=[pltpu.SMEM((planes,), I32)],
        compiler_params=params(),
        name="pack",
    )(unit, rank, counts, plane_of)
    blocks = dict(zip(now, out))
    out = pl.pallas_call(
        lambda *r: repack_kernel([pieces[i] for i in later], *r),
        out_shape=[jax.ShapeDtypeStruct((pieces[i][2], width), BF16) for i in later],
        in_specs=[vmem(), vmem()],
        out_specs=[vmem()] * len(later),
        compiler_params=params(),
        name="repack",
    )(unit, slot)
    blocks |= dict(zip(later, out))

    meta = pl.pallas_call(
        lambda *r: label_kernel(order, cap, *r),
        out_shape=[
            jax.ShapeDtypeStruct((cap, counts.shape[1]), F32),
            jax.ShapeDtypeStruct((1, 2 * planes * cap), F32),
        ],
        in_specs=[vmem(), smem(), smem()],
        out_specs=[vmem()] * 2,
        compiler_params=params(4),
        name="label",
    )(counts, counts, plane_of)
    meta_specs = [vmem()] * 2

    e = f = 3
    own, other, peer = ([None] * n for _ in range(3))
    own[0] = blocks[0]
    own[1] = across_planes(blocks[1], order[1], owners)
    own[2] = across_planes(blocks[2], order[2], owners)
    other[0] = across_sides(own[0], owners)
    other[1] = across_sides(own[1], owners)
    other[2] = across_sides(after(own[2], other[0], other[1]), owners)
    for i in range(e):
        peer[i] = across_subs(after(own[i], own[1]))
    gate = [own[1], meta[0]]
    for i in range(3, n):
        own[i] = across_planes(after(blocks[i], *gate), order[pieces[i][0]], owners)
        other[i] = across_sides(own[i], owners)
        gate = [own[i]] + ([*peer[:e], other[1]] if i == 3 else [])
    for i in range(e, n):
        peer[i] = across_subs(after(own[i], own[-1]) if i < n - 1 else own[i])

    early = pl.pallas_call(
        lambda *r: early_kernel(planes, pieces, e, f, *r),
        out_shape=jax.ShapeDtypeStruct((1, 2 * pieces[e][3]), F32),
        in_specs=meta_specs + [vmem()] * (2 * e + f),
        out_specs=vmem(),
        compiler_params=params(),
        cost_estimate=cost(2 * pieces[e][3], (e + f) * cap, width),
        name="early",
    )(*meta, *own[:e], *other[:f], *peer[:e])
    mine, theirs = pl.pallas_call(
        lambda *r: middle_kernel(planes, pieces, e, f, *r),
        out_shape=[jax.ShapeDtypeStruct((1, planes * cap), F32)] * 2,
        in_specs=meta_specs + [vmem()] * (3 * n),
        out_specs=[vmem()] * 2,
        compiler_params=params(),
        cost_estimate=cost(4 * cap, 6 * cap, width),
        name="middle",
    )(*meta, early, *own, *other[:-1], *peer)
    best = pl.pallas_call(
        lambda *r: last_kernel(planes, cap, pieces, *r),
        out_shape=[jax.ShapeDtypeStruct((1, cap), F32)] * planes,
        in_specs=meta_specs + [vmem()] * (n + 4),
        out_specs=[vmem()] * planes,
        compiler_params=params(),
        name="last",
    )(*meta, mine, across_subs(theirs), *own, other[-1], across_subs(after(other[-1], theirs)))

    back = [best[0]] + [across_planes(best[b], order[b], owners) for b in range(1, planes)]
    return pl.pallas_call(
        lambda *r: place_kernel(planes, cap, *r),
        out_shape=jax.ShapeDtypeStruct((rows,), F32),
        in_specs=[vmem()] * (planes + 1),
        out_specs=vmem(),
        compiler_params=params(8),
        name="place",
    )(slot, *back)


def shards(embeddings, cluster_ids, valid_counts):
    rows, width = embeddings.shape
    owners = lax.axis_size("own")
    planes = owners // 2
    clusters = CL_OWN * owners
    lanes = max(128, 2 * owners)

    share = rows // planes
    caps = sorted({-(-share * k // 12 // 16) * 16 for k in (12, 15, 24)})

    counts, marked = pl.pallas_call(
        count_kernel,
        out_shape=[
            jax.ShapeDtypeStruct((clusters, lanes), I32),
            jax.ShapeDtypeStruct((1, rows), I32),
        ],
        in_specs=[vmem(), vmem()],
        out_specs=[vmem(), vmem()],
        compiler_params=params(2),
        name="count",
    )(cluster_ids, valid_counts)
    counts = lax.psum(counts, ("own", "sub"))
    unit, rank, plane_of, tier = pl.pallas_call(
        lambda *r: unit_kernel(planes, caps, *r),
        out_shape=[
            jax.ShapeDtypeStruct((rows, width), BF16),
            jax.ShapeDtypeStruct((clusters, rows), F32),
            jax.ShapeDtypeStruct((clusters,), I32),
            jax.ShapeDtypeStruct((1,), I32),
        ],
        in_specs=[hbm(), vmem(), vmem()],
        out_specs=[vmem(), vmem(), smem(), smem()],
        scratch_shapes=[pltpu.VMEM((rows, width), BF16), pltpu.SemaphoreType.DMA],
        compiler_params=params(16),
        name="unit",
    )(embeddings, marked, counts)

    def branch(cap):
        return lambda *a: exchange(cap, planes, owners, *a)

    nearest = lax.switch(
        tier[0],
        [branch(cap) for cap in caps],
        unit,
        rank,
        counts,
        plane_of,
    )
    return nearest


def solution(mesh):
    in_specs = (
        P(("groups", "own", "sub"), None),
        P(("groups", "own", "sub")),
        P(("groups", "own", "sub")),
    )
    out_specs = P(("groups", "own", "sub"))
    return jax.shard_map(shards, mesh=mesh, in_specs=in_specs, out_specs=out_specs, check_vma=False)
```

```python
import jax
import jax.numpy as jnp
from jax import lax
from jax.experimental import pallas as pl
from jax.experimental.pallas import tpu as pltpu
from jax.sharding import PartitionSpec as P

CL_OWN = 2
epsilon = 1e-06

F32 = jnp.float32
BF16 = jnp.bfloat16
I32 = jnp.int32


def vmem():
    return pl.BlockSpec(memory_space=pltpu.VMEM)


def smem():
    return pl.BlockSpec(memory_space=pltpu.SMEM)


def hbm():
    return pl.BlockSpec(memory_space=pltpu.HBM)


def group_index():
    return lax.axis_index("own") * 2 + lax.axis_index("sub")


def hits(clusters, marked):
    return marked == lax.broadcasted_iota(I32, (clusters, marked.shape[1]), 0)


def count_kernel(ids_ref, valid_ref, out_ref, marked_ref):
    clusters, lanes = out_ref.shape
    rows = ids_ref.shape[0]
    is_valid = lax.broadcasted_iota(I32, (1, rows), 1) < valid_ref[...].reshape(1, 1)
    marked = jnp.where(is_valid, ids_ref[...].reshape(1, rows), -1)
    marked_ref[...] = marked
    total = jnp.sum(hits(clusters, marked).astype(F32), axis=1, keepdims=True).astype(I32)
    mine = lax.broadcasted_iota(I32, (clusters, lanes), 1) == group_index()
    out_ref[...] = jnp.where(mine, total, 0)


def spread(keys, planes):
    keys = list(keys)
    loads = [F32(0.0)] * planes
    place = [I32(0)] * len(keys)
    for _ in range(len(keys)):
        ranked = [(key, I32(i)) for i, key in enumerate(keys)]
        while len(ranked) > 1:
            ranked = [
                (jnp.maximum(a, b), jnp.where(b > a, bi, ai))
                for (a, ai), (b, bi) in zip(ranked[::2], ranked[1::2])
            ]
        best, best_at = ranked[0]
        ranked = [(load, I32(p)) for p, load in enumerate(loads)]
        while len(ranked) > 1:
            ranked = [
                (jnp.minimum(a, b), jnp.where(b < a, bi, ai))
                for (a, ai), (b, bi) in zip(ranked[::2], ranked[1::2])
            ]
        least_at = ranked[0][1]
        loads = [jnp.where(least_at == p, load + best, load) for p, load in enumerate(loads)]
        place = [jnp.where(best_at == i, least_at, at) for i, at in enumerate(place)]
        keys = [jnp.where(best_at == i, F32(-1.0), key) for i, key in enumerate(keys)]
    return place


def top_load(place, rows, planes):
    top = jnp.zeros_like(rows[0])
    for p in range(planes):
        load = jnp.zeros_like(rows[0])
        for at, row in zip(place, rows):
            load = load + jnp.where(at == p, F32(1.0), F32(0.0)) * row
        top = jnp.maximum(top, load)
    return jnp.max(top)


def plan(planes, caps, counts_ref, plane_ref, tier_ref):
    clusters = counts_ref.shape[0]
    counts = counts_ref[...].astype(F32)
    rows = [counts[c : c + 1] for c in range(clusters)]
    pairs = [rows[c] + rows[c + 1] for c in range(0, clusters, CL_OWN)]

    def settle(place, top):
        for c in range(clusters):
            plane_ref[c] = place[c * len(place) // clusters]
        tier = I32(0)
        for cap in caps[:-1]:
            tier = tier + jnp.where(top > cap, I32(1), I32(0))
        tier_ref[0] = tier

    place = spread([jnp.max(pair) for pair in pairs], planes)
    top = top_load(place, pairs, planes)
    settle(place, top)
    if clusters <= 16:

        @pl.when(top > caps[0])
        def _():
            finer = spread([jnp.sum(row) for row in rows], planes)
            finer_top = top_load(finer, rows, planes)

            @pl.when(finer_top < top)
            def _():
                settle(finer, finer_top)


def unit_kernel(
    planes, caps, emb_ref, marked_ref, counts_ref, unit_ref, rank_ref, plane_ref, tier_ref, wide, sem
):
    copy = pltpu.make_async_copy(emb_ref, wide, sem)
    copy.start()
    clusters = counts_ref.shape[0]
    rows = emb_ref.shape[0]
    hit = hits(clusters, marked_ref[...])
    upto = lax.broadcasted_iota(I32, (rows, rows), 0) <= lax.broadcasted_iota(I32, (rows, rows), 1)
    rank_ref[...] = jnp.where(
        hit,
        jnp.dot(
            hit.astype(F32).astype(BF16),
            upto.astype(F32).astype(BF16),
            preferred_element_type=F32,
        ),
        0.0,
    )
    plan(planes, caps, counts_ref, plane_ref, tier_ref)
    copy.wait()
    x = wide[...].astype(F32)
    unit_ref[...] = (
        x * lax.rsqrt(jnp.sum(x * x, axis=1, keepdims=True) + epsilon)
    ).astype(BF16)


def slot_kernel(order, cap, rank_ref, counts_ref, plane_ref, seen):
    clusters, rows = rank_ref.shape
    me = group_index()
    my_plane = lax.axis_index("own") // 2
    for p in range(len(order)):
        seen[p] = 0
    base = jnp.zeros((clusters, 1), F32)
    at = lax.broadcasted_iota(I32, (clusters, 1), 0)
    for c in range(clusters):
        p = plane_ref[c]
        block = I32(0)
        for b, o in enumerate(order):
            block = jnp.where((p ^ my_plane) == o, I32(b), block)
        first = block * cap + seen[p]
        seen[p] = seen[p] + counts_ref[c, me]
        base = jnp.where(at == c, first.astype(F32), base)
    rank = rank_ref[...]
    slot = jnp.sum(jnp.where(rank > 0.0, rank + base, 0.0), axis=0, keepdims=True)
    return slot.astype(I32) - 1


def pick_rows(pieces, slot, unit_ref, out_refs):
    unit = unit_ref[...]
    for (_, _, size, begin), out_ref in zip(pieces, out_refs):
        at = lax.broadcasted_iota(I32, (size, slot.shape[1]), 0) + begin
        pick = (slot == at).astype(F32).astype(BF16)
        out_ref[...] = jnp.dot(pick, unit, preferred_element_type=F32).astype(BF16)


def pack_kernel(order, cap, pieces, unit_ref, rank_ref, counts_ref, plane_ref, *refs):
    *out_refs, slot_ref, seen = refs
    slot = slot_kernel(order, cap, rank_ref, counts_ref, plane_ref, seen)
    slot_ref[...] = slot
    pick_rows(pieces, slot, unit_ref, out_refs)


def repack_kernel(pieces, unit_ref, slot_ref, *out_refs):
    pick_rows(pieces, slot_ref[...], unit_ref, out_refs)


def source(k, o):
    plane, side = lax.axis_index("own") // 2, lax.axis_index("own") % 2
    return ((plane ^ o) * 2 + (side ^ (k & 1))) * 2 + (lax.axis_index("sub") ^ (k >> 1))


def label_kernel(order, cap, counts_ref, cnt_ref, plane_ref, keys_ref, queries_ref):
    clusters, lanes = counts_ref.shape
    my_plane = lax.axis_index("own") // 2
    counts = counts_ref[...]
    row_at = lax.broadcasted_iota(I32, (cap, lanes), 0)
    lane_at = lax.broadcasted_iota(I32, (cap, lanes), 1)
    slot_at = lax.broadcasted_iota(I32, (1, cap), 1)
    key_total = jnp.zeros((1, lanes), I32)
    key_label = jnp.zeros((cap, lanes), F32)
    devices = [source(k, o) for k in (0, 2) for o in order]
    query_total = [I32(0)] * len(devices)
    query_label = [jnp.zeros((1, cap), F32)] * len(devices)
    for c in range(clusters):
        here = plane_ref[c] == my_plane
        key_total = key_total + jnp.where(here, counts[c : c + 1], 0)
        key_label = key_label + jnp.where(row_at >= key_total, 1.0, 0.0)
        for i, device in enumerate(devices):
            query_total[i] = query_total[i] + jnp.where(here, cnt_ref[c, device], 0)
            query_label[i] = query_label[i] + jnp.where(slot_at >= query_total[i], 1.0, 0.0)
    queries_ref[...] = jnp.concatenate(query_label, axis=1)
    columns = jnp.zeros((cap, lanes), F32)
    for k in range(4):
        for b, o in enumerate(order):
            one = jnp.where(lane_at == source(k, o), key_label, 0.0)
            one = jnp.sum(one, axis=1, keepdims=True)
            columns = jnp.where(lane_at == k * len(order) + b, one, columns)
    keys_ref[...] = columns


def fold(best, scores, key_label, query_label, distance):
    same = key_label == query_label
    if distance is not None:
        size, width = scores.shape
        same = same & (
            lax.broadcasted_iota(I32, (size, width), 0) + distance
            != lax.broadcasted_iota(I32, (size, width), 1)
        )
    masked = jnp.where(same, scores, -1.0)
    size, width = scores.shape
    return jnp.maximum(best, jnp.max(masked.reshape(size // 8, 8, width), axis=0))


def score(a, b):
    return lax.dot_general(a, b, (((1,), (1,)), ((), ())), preferred_element_type=F32)


def gather(refs):
    return jnp.concatenate([ref[...] for ref in refs], axis=0)


def fold_pieces(best, scores, keys_ref, planes, parts, query_label):
    at = 0
    for (b, start, size, begin), k, among in parts:
        best = fold(
            best,
            scores[at : at + size],
            keys_ref[start : start + size, k * planes + b : k * planes + b + 1],
            query_label,
            begin if among else None,
        )
        at += size
    return jnp.max(best, axis=0, keepdims=True)


def early_kernel(planes, pieces, e, f, keys_ref, queries_ref, *refs):
    own, other, peer, out_ref = refs[:e], refs[e : e + f], refs[e + f : 2 * e + f], refs[-1]
    rows = gather(own)
    edge, total = rows.shape[0], queries_ref.shape[1] // 2
    label = queries_ref[...]
    label = jnp.concatenate([label[:, :edge], label[:, total : total + edge]], axis=1)
    queries = jnp.concatenate([rows, gather(peer)], axis=0)
    scores = score(jnp.concatenate([rows, gather(other)], axis=0), queries)
    parts = [(piece, 0, True) for piece in pieces[:e]] + [(piece, 1, False) for piece in pieces[:f]]
    best = jnp.full((8, 2 * edge), -1.0, F32)
    out_ref[...] = fold_pieces(best, scores, keys_ref, planes, parts, label)


def middle_kernel(planes, pieces, e, f, keys_ref, queries_ref, early_ref, *refs):
    n = len(pieces)
    own, other, peer = refs[:n], refs[n : 2 * n - 1], refs[2 * n - 1 : 3 * n - 1]
    mine_ref, theirs_ref = refs[3 * n - 1 :]
    rows, peers = gather(own), gather(peer)
    width, edge = rows.shape[0], pieces[e][3]
    label = queries_ref[...]
    late_label = jnp.concatenate([label[:, edge:width], label[:, width + edge :]], axis=1)
    queries = jnp.concatenate([rows[edge:], peers[edge:]], axis=0)
    scores = score(jnp.concatenate([rows[:edge], gather(other[:f])], axis=0), queries)
    parts = [(piece, 0, False) for piece in pieces[:e]]
    parts += [(piece, 1, False) for piece in pieces[:f]]
    late = jnp.full((8, 2 * (width - edge)), -1.0, F32)
    late = fold_pieces(late, scores, keys_ref, planes, parts, late_label)

    queries = jnp.concatenate([rows, peers], axis=0)
    held = jnp.concatenate([rows[edge:], *[ref[...] for ref in other[f:]]], axis=0)
    parts = [(piece, 0, True) for piece in pieces[e:]]
    parts += [(piece, 1, False) for piece in pieces[f : n - 1]]
    best = jnp.full((8, 2 * width), -1.0, F32)
    best = fold_pieces(best, score(held, queries), keys_ref, planes, parts, label)
    early = early_ref[...]
    for k, out_ref in enumerate((mine_ref, theirs_ref)):
        out_ref[:, :edge] = jnp.maximum(
            best[:, k * width : k * width + edge], early[:, k * edge : (k + 1) * edge]
        )
        out_ref[:, edge:] = jnp.maximum(
            best[:, k * width + edge : (k + 1) * width],
            late[:, k * (width - edge) : (k + 1) * (width - edge)],
        )


def last_kernel(planes, cap, pieces, keys_ref, queries_ref, mine_ref, theirs_ref, *refs):
    n = len(pieces)
    own, keys, out_refs = refs[:n], refs[n : n + 2], refs[n + 2 :]
    rows = gather(own)
    width = rows.shape[0]
    best = jnp.full((8, width), -1.0, F32)
    parts = [(pieces[-1], 1, False), (pieces[-1], 3, False)]
    label = queries_ref[:, :width]
    best = fold_pieces(best, score(gather(keys), rows), keys_ref, planes, parts, label)
    best = jnp.maximum(best, jnp.maximum(mine_ref[...], theirs_ref[...]))
    for b in range(planes):
        out_refs[b][...] = best[:, b * cap : (b + 1) * cap]


def place_kernel(planes, cap, slot_ref, *refs):
    back_refs, out_ref = refs[:planes], refs[planes]
    rows = slot_ref.shape[1]
    slot = slot_ref[...]
    part = jnp.zeros((1, rows), I32)
    for o in range(1, planes):
        part = part + jnp.where(slot >= o * cap, 1, 0)
    inner = slot - part * cap
    pick = (inner == lax.broadcasted_iota(I32, (cap, rows), 0)).astype(F32).astype(BF16)
    rest = jnp.concatenate([ref[...] for ref in back_refs], axis=0)
    found = jnp.zeros((planes, rows), F32)
    for _ in range(3):
        head = rest.astype(BF16)
        rest = rest - head.astype(F32)
        found = found + jnp.dot(head, pick, preferred_element_type=F32)
    chosen = part == lax.broadcasted_iota(I32, (planes, rows), 0)
    found = jnp.sum(jnp.where(chosen, found, 0.0), axis=0, keepdims=True)
    out_ref[...] = jnp.where(slot >= 0, found, 0.0).reshape(rows)


def params(limit=24):
    return pltpu.CompilerParams(vmem_limit_bytes=limit * 1024 * 1024)


def cost(rows, columns, depth):
    return pl.CostEstimate(
        flops=2 * rows * columns * depth,
        bytes_accessed=2 * (rows + columns) * depth,
        transcendentals=0,
    )


def after(x, *y):
    return lax.optimization_barrier((x, *y))[0] if y else x


def across_planes(x, offset, owners, side=0):
    return lax.ppermute(x, "own", [(a, a ^ (2 * offset + side)) for a in range(owners)])


def across_sides(x, owners):
    return lax.ppermute(x, "own", [(a, a ^ 1) for a in range(owners)])


def across_subs(x):
    return lax.ppermute(x, "sub", [(0, 1), (1, 0)])


def exchange(cap, planes, owners, unit, rank, counts, plane_of):
    rows, width = unit.shape
    tail = -(-cap // 48) * 16
    half, last = planes // 2, planes - 1
    order = [0, half, *range(1, half), *range(half + 1, planes)]
    pieces = [(b, 0, cap, b * cap) for b in range(last)]
    pieces += [
        (last, 0, cap - tail, last * cap),
        (last, cap - tail, tail, (last + 1) * cap - tail),
    ]
    n = len(pieces)

    now, later = [1], [i for i in range(n) if i != 1]
    *out, slot = pl.pallas_call(
        lambda *r: pack_kernel(order, cap, [pieces[i] for i in now], *r),
        out_shape=[jax.ShapeDtypeStruct((pieces[i][2], width), BF16) for i in now]
        + [jax.ShapeDtypeStruct((1, rows), I32)],
        in_specs=[vmem(), vmem(), smem(), smem()],
        out_specs=[vmem()] * (len(now) + 1),
        scratch_shapes=[pltpu.SMEM((planes,), I32)],
        compiler_params=params(),
        name="pack",
    )(unit, rank, counts, plane_of)
    blocks = dict(zip(now, out))
    out = pl.pallas_call(
        lambda *r: repack_kernel([pieces[i] for i in later], *r),
        out_shape=[jax.ShapeDtypeStruct((pieces[i][2], width), BF16) for i in later],
        in_specs=[vmem(), vmem()],
        out_specs=[vmem()] * len(later),
        compiler_params=params(),
        name="repack",
    )(unit, slot)
    blocks |= dict(zip(later, out))

    meta = pl.pallas_call(
        lambda *r: label_kernel(order, cap, *r),
        out_shape=[
            jax.ShapeDtypeStruct((cap, counts.shape[1]), F32),
            jax.ShapeDtypeStruct((1, 2 * planes * cap), F32),
        ],
        in_specs=[vmem(), smem(), smem()],
        out_specs=[vmem()] * 2,
        compiler_params=params(4),
        name="label",
    )(counts, counts, plane_of)
    meta_specs = [vmem()] * 2

    e = f = 3
    own, other, peer = ([None] * n for _ in range(3))
    own[0] = blocks[0]
    own[1] = across_planes(blocks[1], order[1], owners)
    own[2] = across_planes(blocks[2], order[2], owners)
    other[0] = across_sides(own[0], owners)
    other[1] = across_sides(own[1], owners)
    other[2] = across_sides(after(own[2], other[0], other[1]), owners)
    for i in range(e):
        peer[i] = across_subs(after(own[i], own[1]))
    gate = [own[1], meta[0]]
    for i in range(3, n):
        own[i] = across_planes(after(blocks[i], *gate), order[pieces[i][0]], owners)
        other[i] = across_sides(own[i], owners)
        gate = [own[i]] + ([*peer[:e], other[1]] if i == 3 else [])
    for i in range(e, n):
        peer[i] = across_subs(after(own[i], own[-1]) if i < n - 1 else own[i])

    early = pl.pallas_call(
        lambda *r: early_kernel(planes, pieces, e, f, *r),
        out_shape=jax.ShapeDtypeStruct((1, 2 * pieces[e][3]), F32),
        in_specs=meta_specs + [vmem()] * (2 * e + f),
        out_specs=vmem(),
        compiler_params=params(),
        cost_estimate=cost(2 * pieces[e][3], (e + f) * cap, width),
        name="early",
    )(*meta, *own[:e], *other[:f], *peer[:e])
    mine, theirs = pl.pallas_call(
        lambda *r: middle_kernel(planes, pieces, e, f, *r),
        out_shape=[jax.ShapeDtypeStruct((1, planes * cap), F32)] * 2,
        in_specs=meta_specs + [vmem()] * (3 * n),
        out_specs=[vmem()] * 2,
        compiler_params=params(),
        cost_estimate=cost(4 * cap, 6 * cap, width),
        name="middle",
    )(*meta, early, *own, *other[:-1], *peer)
    best = pl.pallas_call(
        lambda *r: last_kernel(planes, cap, pieces, *r),
        out_shape=[jax.ShapeDtypeStruct((1, cap), F32)] * planes,
        in_specs=meta_specs + [vmem()] * (n + 4),
        out_specs=[vmem()] * planes,
        compiler_params=params(),
        name="last",
    )(*meta, mine, across_subs(theirs), *own, other[-1], across_subs(after(other[-1], theirs)))

    back = [best[0]] + [across_planes(best[b], order[b], owners) for b in range(1, planes)]
    return pl.pallas_call(
        lambda *r: place_kernel(planes, cap, *r),
        out_shape=jax.ShapeDtypeStruct((rows,), F32),
        in_specs=[vmem()] * (planes + 1),
        out_specs=vmem(),
        compiler_params=params(8),
        name="place",
    )(slot, *back)


def shards(embeddings, cluster_ids, valid_counts):
    rows, width = embeddings.shape
    owners = lax.axis_size("own")
    planes = owners // 2
    clusters = CL_OWN * owners
    lanes = max(128, 2 * owners)

    share = rows // planes
    caps = sorted({-(-share * k // 12 // 16) * 16 for k in (12, 15, 24)})

    counts, marked = pl.pallas_call(
        count_kernel,
        out_shape=[
            jax.ShapeDtypeStruct((clusters, lanes), I32),
            jax.ShapeDtypeStruct((1, rows), I32),
        ],
        in_specs=[vmem(), vmem()],
        out_specs=[vmem(), vmem()],
        compiler_params=params(2),
        name="count",
    )(cluster_ids, valid_counts)
    counts = lax.psum(counts, ("own", "sub"))
    unit, rank, plane_of, tier = pl.pallas_call(
        lambda *r: unit_kernel(planes, caps, *r),
        out_shape=[
            jax.ShapeDtypeStruct((rows, width), BF16),
            jax.ShapeDtypeStruct((clusters, rows), F32),
            jax.ShapeDtypeStruct((clusters,), I32),
            jax.ShapeDtypeStruct((1,), I32),
        ],
        in_specs=[hbm(), vmem(), vmem()],
        out_specs=[vmem(), vmem(), smem(), smem()],
        scratch_shapes=[pltpu.VMEM((rows, width), BF16), pltpu.SemaphoreType.DMA],
        compiler_params=params(16),
        name="unit",
    )(embeddings, marked, counts)

    def branch(cap):
        return lambda *a: exchange(cap, planes, owners, *a)

    nearest = lax.switch(
        tier[0],
        [branch(cap) for cap in caps],
        unit,
        rank,
        counts,
        plane_of,
    )
    return nearest


def solution(mesh):
    in_specs = (
        P(("groups", "own", "sub"), None),
        P(("groups", "own", "sub")),
        P(("groups", "own", "sub")),
    )
    out_specs = P(("groups", "own", "sub"))
    return jax.shard_map(shards, mesh=mesh, in_specs=in_specs, out_specs=out_specs, check_vma=False)
```
